32 devices in a mesh: section: 8 (over z, core), blk: 4 (over y, x).
Axes of the slice: x: 2, y: 2, z: 4, core: 2. Of those that a mesh axis runs over, the one named last changes fastest.
Arguments:
- held_input: bfloat16 [8, 5120, 128], P('section', 'blk'), may hold values from -6 to 6
- fresh_input: bfloat16 [5120, 128], P('blk'), may hold values from -6 to 6
- stashed: bfloat16 [8, 2, 5120, 128], P('section', None, 'blk'), may hold values from -6 to 6
- held_grad: bfloat16 [8, 5120, 128], P('section', 'blk'), may hold values from -6 to 6
- fresh_grad: bfloat16 [5120, 128], P('blk'), may hold values from -6 to 6
- first_up: bfloat16 [8, 2, 128, 6400], P('section', None, 'blk'), may hold values from -1 to 1
- second_up: bfloat16 [8, 2, 160, 16384], P('section', None, 'blk'), may hold values from -0.5 to 0.5
- first_down: bfloat16 [8, 160, 16384], P('section', 'blk'), may hold values from -0.5 to 0.5
- second_down: bfloat16 [8, 128, 6400], P('section', 'blk'), may hold values from -0.5 to 0.5
Outputs:
- passed_output: bfloat16 [8, 5120, 128], P('section', 'blk')
- passed_grad: bfloat16 [8, 5120, 128], P('section', 'blk')
- grad_first_up: bfloat16 [8, 2, 128, 6400], P('section', None, 'blk')
- grad_second_up: bfloat16 [8, 2, 160, 16384], P('section', None, 'blk')
- grad_first_down: bfloat16 [8, 160, 16384], P('section', 'blk')
- grad_second_down: bfloat16 [8, 128, 6400], P('section', 'blk')
The draws below stay inside these ranges and needn't reach their ends.
All inputs are finite; a program needn't handle non-finite values.
Results may differ from the reference program's by a relative error of at most 0.0095.
Values may be sent and summed in bfloat16 or wider, within the bound.
A program may use at most 128 MiB of HBM per device.

```python
import math
import jax
import jax.numpy as jnp
from jax import lax

D = 5120
BLOCK = 128
FIRST_BLOCKS = 128
FIRST_IN = 40
SECOND_BLOCKS = 160
MB_TOK = 128
TICKS = 2
N_SECTION = 8


def levels(own_key, dims, shards, smallest, largest):
    loudness = 1.0
    for axis_at, shards_of in shards:
        heights = jax.random.uniform(jax.random.fold_in(jax.random.fold_in(own_key, 6), axis_at), (shards_of,), jnp.float32, smallest / len(shards), largest / len(shards))
        loudness = loudness * jnp.repeat(jnp.exp(heights), dims[axis_at] // shards_of).reshape((-1,) + (1,) * (len(dims) - 1 - axis_at))
    return loudness


def noise(own_key, dims, deviation, most, split=(), held_as=jnp.bfloat16):
    array = deviation * jax.random.normal(own_key, dims, jnp.float32)
    if split:
        array = array * levels(own_key, dims, split, -0.22, 0.18)
    return jnp.clip(array, -most, most).astype(held_as)


def setup_inputs(seed: int = 0) -> dict:
    arg_keys = jax.random.split(jax.random.key(seed), 10)
    held_input = noise(arg_keys[0], (N_SECTION, D, MB_TOK), 1.0, 6.0, ((0, 8), (1, 4)))
    fresh_input = noise(arg_keys[1], (D, MB_TOK), 1.0, 6.0, ((0, 4),))
    stashed = noise(arg_keys[2], (N_SECTION, TICKS, D, MB_TOK), 1.0, 6.0, ((0, 8), (2, 4)))
    held_grad = noise(arg_keys[3], (N_SECTION, D, MB_TOK), 1.0, 6.0, ((0, 8), (1, 4)))
    fresh_grad = noise(arg_keys[4], (D, MB_TOK), 1.0, 6.0, ((0, 4),))
    first_up = noise(arg_keys[5], (N_SECTION, 2, FIRST_BLOCKS, FIRST_IN * SECOND_BLOCKS), FIRST_IN ** -0.5, 1.0, ((0, 8), (2, 4)))
    second_up = noise(arg_keys[6], (N_SECTION, 2, SECOND_BLOCKS, FIRST_BLOCKS * BLOCK), FIRST_BLOCKS ** -0.5, 0.5, ((0, 8), (2, 4)))
    first_down = noise(arg_keys[7], (N_SECTION, SECOND_BLOCKS, BLOCK * FIRST_BLOCKS), BLOCK ** -0.5, 0.5, ((0, 8), (1, 4)))
    second_down = noise(arg_keys[8], (N_SECTION, FIRST_BLOCKS, SECOND_BLOCKS * FIRST_IN), SECOND_BLOCKS ** -0.5, 0.5, ((0, 8), (1, 4)))
    return dict(held_input=held_input, fresh_input=fresh_input, stashed=stashed, held_grad=held_grad, fresh_grad=fresh_grad, first_up=first_up, second_up=second_up, first_down=first_down, second_down=second_down)


def layer_tick(inputs, cotangent, stash, first_up, second_up, first_down, second_down):
    tokens = inputs.shape[1]
    up_first = first_up.reshape(2, FIRST_BLOCKS, FIRST_IN, SECOND_BLOCKS).astype(jnp.float32)
    up_second = second_up.reshape(2, SECOND_BLOCKS, FIRST_BLOCKS, BLOCK).astype(jnp.float32)
    down_first = first_down.reshape(SECOND_BLOCKS, BLOCK, FIRST_BLOCKS).astype(jnp.float32)
    down_second = second_down.reshape(FIRST_BLOCKS, SECOND_BLOCKS, FIRST_IN).astype(jnp.float32)

    def forward(source):
        values = source.reshape(FIRST_BLOCKS, FIRST_IN, tokens).astype(jnp.float32)
        spread = jnp.einsum('pqt,gpqr->gprt', values, up_first).astype(jnp.bfloat16)
        mixed = jnp.einsum('gprt,grpo->grot', spread.astype(jnp.float32), up_second)
        hidden = (jax.nn.silu(mixed[0]) * mixed[1]).astype(jnp.bfloat16)
        lowered = jnp.einsum('rot,rop->rpt', hidden.astype(jnp.float32), down_first).astype(jnp.bfloat16)
        result = values + jnp.einsum('rpt,prq->pqt', lowered.astype(jnp.float32), down_second)
        return (values, spread, mixed, hidden, lowered, result.astype(jnp.bfloat16))
    produced = forward(inputs)[5].reshape(D, tokens)
    values, spread, mixed, hidden, lowered, unused = forward(stash)
    grads = cotangent.reshape(FIRST_BLOCKS, FIRST_IN, tokens).astype(jnp.float32)
    grad_lowered = jnp.einsum('pqt,prq->prt', grads, down_second).astype(jnp.bfloat16)
    grad_hidden = jnp.einsum('prt,rop->rot', grad_lowered.astype(jnp.float32), down_first)
    sigmoid_gate = jax.nn.sigmoid(mixed[0])
    slope = sigmoid_gate * (1.0 + mixed[0] * (1.0 - sigmoid_gate))
    grad_mixed = jnp.stack([grad_hidden * mixed[1] * slope, grad_hidden * mixed[0] * sigmoid_gate]).astype(jnp.bfloat16)
    grad_spread = jnp.einsum('grot,grpo->grpt', grad_mixed.astype(jnp.float32), up_second).astype(jnp.bfloat16)
    back = grads + jnp.einsum('grpt,gpqr->pqt', grad_spread.astype(jnp.float32), up_first)
    term_first_up = jnp.einsum('pqt,grpt->gpqr', values, grad_spread.astype(jnp.float32))
    term_second_up = jnp.einsum('gprt,grot->grpo', spread.astype(jnp.float32), grad_mixed.astype(jnp.float32))
    term_first_down = jnp.einsum('rot,prt->rop', hidden.astype(jnp.float32), grad_lowered.astype(jnp.float32))
    term_second_down = jnp.einsum('rpt,pqt->prq', lowered.astype(jnp.float32), grads)
    return (produced, back.astype(jnp.bfloat16).reshape(D, tokens), term_first_up.reshape(first_up.shape), term_second_up.reshape(second_up.shape), term_first_down.reshape(first_down.shape), term_second_down.reshape(second_down.shape))

def one_section(operands):
    return layer_tick(operands[0], operands[1], operands[2], operands[3], operands[4], operands[5], operands[6])

def reference(held_input, fresh_input, stashed, held_grad, fresh_grad, first_up, second_up, first_down, second_down):
    inputs = held_input
    cotangent = held_grad
    totals = [jnp.zeros(weight.shape, jnp.float32) for weight in (first_up, second_up, first_down, second_down)]
    outputs = held_input
    backward = held_grad
    for tick_index in range(TICKS):
        results = lax.map(one_section, (inputs, cotangent, stashed[:, tick_index], first_up, second_up, first_down, second_down))
        outputs = results[0]
        backward = results[1]
        totals = [totals[number] + results[number + 2] for number in range(4)]
        if tick_index + 1 < TICKS:
            inputs = jnp.concatenate([fresh_input[None], outputs[:-1]], axis=0)
            cotangent = jnp.concatenate([backward[1:], fresh_grad[None]], axis=0)
    factor = 1.0 / math.sqrt(TICKS * MB_TOK)
    return (outputs, backward, (totals[0] * factor).astype(jnp.bfloat16), (totals[1] * factor).astype(jnp.bfloat16), (totals[2] * factor).astype(jnp.bfloat16), (totals[3] * factor).astype(jnp.bfloat16))
```

```python
import math

import jax
import jax.numpy as jnp
from jax import lax
from jax.sharding import PartitionSpec as P

FIRST_BLOCKS = 128
FIRST_IN = 40
SECOND_BLOCKS = 160
TICKS = 2
JOIN = 8
F32 = jnp.float32
BF16 = jnp.bfloat16


def from_behind(value, axis, by):
    length = lax.axis_size(axis)
    pairs = [(i, i + by) for i in range(length) if 0 <= i + by < length]
    return lax.ppermute(value, axis, pairs)


def partner_of(i, d, n):
    return i ^ d if n & (n - 1) == 0 else (i + d) % n


def sum_scatter(pieces, n, me):
    total = lax.dynamic_index_in_dim(pieces, me, 0, keepdims=False).astype(F32)
    for d in range(1, n):
        mine = lax.dynamic_index_in_dim(pieces, partner_of(me, d, n), 0, keepdims=False)
        total = total + lax.ppermute(
            mine, "blk", [(i, partner_of(i, d, n)) for i in range(n)]
        ).astype(F32)
    return total


def shards(
    held_input,
    fresh_input,
    stashed,
    held_grad,
    fresh_grad,
    first_up,
    second_up,
    first_down,
    second_down,
):
    n = lax.axis_size("blk")
    me = lax.axis_index("blk")
    section_pos = lax.axis_index("section")
    last_section = lax.axis_size("section") - 1
    own_p = FIRST_BLOCKS // n
    own_r = SECOND_BLOCKS // n
    own_groups = own_p // JOIN
    groups = FIRST_BLOCKS // JOIN
    width = JOIN * FIRST_IN
    rows, tokens = held_input.shape[1:]

    def gather(value):
        return lax.all_gather(value, "blk", axis=0, tiled=True)

    up_cut = first_up[0].reshape(2, own_groups, JOIN, FIRST_IN, n, own_r).transpose(4, 1, 0, 5, 2, 3)
    down_cut = second_down[0].reshape(own_groups, JOIN, n, own_r, FIRST_IN).transpose(2, 0, 3, 1, 4)
    cut = jnp.concatenate(
        [
            up_cut.reshape(n, own_groups, 2, own_r, width),
            down_cut.reshape(n, own_groups, 1, own_r, width),
        ],
        axis=2,
    )
    cut = lax.optimization_barrier(cut)
    factors = lax.all_to_all(cut, "blk", split_axis=0, concat_axis=0, tiled=True)
    factors = factors.reshape(groups, 3, own_r, 1, width)
    same = (lax.broadcasted_iota(jnp.int32, (JOIN, width), 1) // FIRST_IN) == lax.broadcasted_iota(
        jnp.int32, (JOIN, width), 0
    )
    factors = lax.optimization_barrier(factors)
    up_wide = jnp.where(same, factors[:, :2], jnp.zeros((), BF16))
    down_wide = jnp.where(same, factors[:, 2], jnp.zeros((), BF16))
    up_wide, down_wide = lax.optimization_barrier(
        (
            up_wide.reshape(groups, 2 * own_r * JOIN, width),
            down_wide.reshape(groups, own_r * JOIN, width),
        )
    )
    up_second = second_up[0].reshape(2, own_r, FIRST_BLOCKS, -1)
    down_first = first_down[0].reshape(own_r, -1, FIRST_BLOCKS)

    def by_r(wide, values):
        t = values.shape[1]
        out = jnp.einsum(
            "gak,gkt->gat", wide, values.reshape(groups, width, t), preferred_element_type=F32
        ).astype(BF16)
        out = out.reshape(groups, -1, JOIN, t).transpose(1, 0, 2, 3)
        return out.reshape(-1, FIRST_BLOCKS, t)

    def by_p(wide, values):
        t = values.shape[2]
        v = values.reshape(-1, groups, JOIN, t).transpose(1, 0, 2, 3).reshape(groups, -1, t)
        out = jnp.einsum("gak,gat->gkt", wide, v, preferred_element_type=F32).astype(BF16)
        return out.reshape(n, rows, t)

    def middle(values):
        t = values.shape[1]
        spread = by_r(up_wide, values).reshape(2, own_r, FIRST_BLOCKS, t)
        mixed = jnp.einsum("grpo,grpt->grot", up_second, spread, preferred_element_type=F32)
        hidden = (jax.nn.silu(mixed[0]) * mixed[1]).astype(BF16)
        lowered = jnp.einsum("rop,rot->rpt", down_first, hidden, preferred_element_type=F32)
        return spread, mixed, hidden, lowered.astype(BF16)

    def forward(values, values_all):
        lowered = middle(values_all)[3]
        added = sum_scatter(by_p(down_wide, lowered), n, me)
        return (values.astype(F32) + added).astype(BF16)

    def backward(grads, grads_all, mixed):
        grad_lowered = by_r(down_wide, grads_all)
        grad_hidden = jnp.einsum(
            "rop,rpt->rot", down_first, grad_lowered, preferred_element_type=F32
        )
        sg = jax.nn.sigmoid(mixed[0])
        slope = sg * (1.0 + mixed[0] * (1.0 - sg))
        grad_mixed = jnp.stack(
            [grad_hidden * mixed[1] * slope, grad_hidden * mixed[0] * sg]
        ).astype(BF16)
        grad_spread = jnp.einsum(
            "grpo,grot->grpt", up_second, grad_mixed, preferred_element_type=F32
        ).astype(BF16)
        added = sum_scatter(by_p(up_wide, grad_spread.reshape(-1, FIRST_BLOCKS, tokens)), n, me)
        return (grads.astype(F32) + added).astype(BF16), grad_lowered, grad_mixed, grad_spread

    inputs, grads = held_input[0], held_grad[0]
    inputs_all = gather(inputs)
    grads_all = gather(grads)
    stash_all = gather(jnp.concatenate([stashed[0, k] for k in range(TICKS)], axis=1))
    spread, mixed, hidden, lowered = middle(stash_all)
    terms, grads_seen = [], []
    outputs = back = None
    for k in range(TICKS):
        outputs = forward(inputs, inputs_all)
        back, *term = backward(grads, grads_all, mixed[..., k * tokens : (k + 1) * tokens])
        terms.append(term)
        grads_seen.append(grads_all)
        if k + 1 < TICKS:
            inputs = jnp.where(section_pos == 0, fresh_input, from_behind(outputs, "section", 1))
            grads = jnp.where(
                section_pos == last_section, fresh_grad, from_behind(back, "section", -1)
            )
            inputs_all = gather(inputs)
            grads_all = gather(grads)
    grad_lowered, grad_mixed, grad_spread = (
        jnp.concatenate([term[i] for term in terms], axis=-1) for i in range(3)
    )
    both = jnp.concatenate(grads_seen, axis=1)
    factor = 1.0 / math.sqrt(TICKS * tokens)

    def finish(total):
        return (total * factor).astype(BF16)

    w2 = finish(jnp.einsum("grpt,grot->grpo", spread, grad_mixed, preferred_element_type=F32))
    w3 = finish(jnp.einsum("rot,rpt->rop", hidden, grad_lowered, preferred_element_type=F32))
    stash_blocks = stash_all.reshape(FIRST_BLOCKS, FIRST_IN, -1)
    w1 = finish(
        jnp.einsum("grpt,pqt->pgrq", grad_spread, stash_blocks, preferred_element_type=F32)
    )
    w4 = finish(
        jnp.einsum(
            "rpt,pqt->prq",
            lowered,
            both.reshape(FIRST_BLOCKS, FIRST_IN, -1),
            preferred_element_type=F32,
        )
    )
    back_cut = jnp.concatenate([w1, w4[:, None]], axis=1).reshape(n, own_p, 3, own_r, FIRST_IN)
    small = lax.all_to_all(back_cut, "blk", split_axis=0, concat_axis=0, tiled=True)
    g1 = small[:, :, :2].transpose(2, 1, 4, 0, 3)
    g4 = small[:, :, 2].transpose(1, 0, 2, 3)
    return (
        outputs.reshape(held_input.shape),
        back.reshape(held_grad.shape),
        g1.reshape(first_up.shape),
        w2.reshape(second_up.shape),
        w3.reshape(first_down.shape),
        g4.reshape(second_down.shape),
    )


def solution(mesh):
    return jax.shard_map(
        shards,
        mesh=mesh,
        in_specs=(
            P("section", "blk", None),
            P("blk", None),
            P("section", None, "blk", None),
            P("section", "blk", None),
            P("blk", None),
            P("section", None, "blk", None),
            P("section", None, "blk", None),
            P("section", "blk", None),
            P("section", "blk", None),
        ),
        out_specs=(
            P("section", "blk", None),
            P("section", "blk", None),
            P("section", None, "blk", None),
            P("section", None, "blk", None),
            P("section", "blk", None),
            P("section", "blk", None),
        ),
        check_vma=False,
    )
```

```python
import functools
import math

import jax
import jax.numpy as jnp
from jax import lax
from jax.experimental import pallas as pl
from jax.experimental.pallas import tpu as pltpu
from jax.sharding import PartitionSpec as P

FIRST_BLOCKS = 128
FIRST_IN = 40
SECOND_BLOCKS = 160
PAIR = 2
TICKS = 2
JOIN = 8
F32 = jnp.float32
BF16 = jnp.bfloat16


def from_behind(value, axis, by):
    length = lax.axis_size(axis)
    pairs = [(i, i + by) for i in range(length) if 0 <= i + by < length]
    return lax.ppermute(value, axis, pairs)


def partner_of(i, d, n):
    return i ^ d if n & (n - 1) == 0 else (i + d) % n


def send(pieces, n, me):
    arrived = [lax.dynamic_index_in_dim(pieces, me, 0, keepdims=False)]
    for d in range(1, n):
        mine = lax.dynamic_index_in_dim(pieces, partner_of(me, d, n), 0, keepdims=False)
        arrived.append(
            lax.ppermute(mine, "blk", [(i, partner_of(i, d, n)) for i in range(n)])
        )
    return arrived


def total_of(pieces):
    return sum(piece.astype(F32) for piece in pieces)


def wide_of(factor):
    a, width = factor.shape
    block = lax.broadcasted_iota(jnp.int32, (JOIN, width), 0) * FIRST_IN
    column = lax.broadcasted_iota(jnp.int32, (JOIN, width), 1)
    keep = (column >= block) & (column < block + FIRST_IN)
    spread = jnp.broadcast_to(factor.astype(F32)[:, None, :], (a, JOIN, width))
    return jnp.where(keep[None], spread, 0.0).reshape(a * JOIN, width)


def by_r_kernel(factor_ref, values_ref, out_ref):
    a = factor_ref.shape[1]
    t = values_ref.shape[2]
    parts = []
    for i in range(PAIR):
        wide = wide_of(factor_ref[i]).astype(BF16)
        out = jnp.dot(wide, values_ref[i], preferred_element_type=F32)
        parts.append(out.reshape(a, JOIN, t))
    out_ref[...] = jnp.concatenate(parts, axis=1).astype(BF16)


def by_p_kernel(factor_ref, rows_ref, out_ref):
    rows = rows_ref[...].astype(F32)
    a, _, t = rows.shape
    for i in range(PAIR):
        wide = wide_of(factor_ref[i]).astype(BF16)
        mine = rows[:, i * JOIN : (i + 1) * JOIN].reshape(a * JOIN, t).astype(BF16)
        out = lax.dot_general(wide, mine, (((0,), (0,)), ((), ())), preferred_element_type=F32)
        out_ref[i] = out.astype(BF16)


def term_kernel(factor, rows_ref, values_ref, out_ref):
    rows = rows_ref[...].astype(F32)
    a, _, t = rows.shape
    width = values_ref.shape[1]
    block = lax.broadcasted_iota(jnp.int32, (JOIN, width), 0) * FIRST_IN
    column = lax.broadcasted_iota(jnp.int32, (JOIN, width), 1)
    keep = (column >= block) & (column < block + FIRST_IN)
    for i in range(PAIR):
        mine = rows[:, i * JOIN : (i + 1) * JOIN].reshape(a * JOIN, t).astype(BF16)
        full = lax.dot_general(
            mine, values_ref[i], (((1,), (1,)), ((), ())), preferred_element_type=F32
        )
        kept = jnp.where(keep[None], full.reshape(a, JOIN, width), 0.0)
        out_ref[i] = (jnp.sum(kept, axis=1) * factor).astype(BF16)


def call(kernel, flops, out_dims, out_block, out_map, operands, blocks, maps):
    moved = sum(x.size for x in operands) * 2 + math.prod(out_dims) * 2
    return pl.pallas_call(
        kernel,
        grid=(FIRST_BLOCKS // (PAIR * JOIN),),
        in_specs=[pl.BlockSpec(x, m) for x, m in zip(blocks, maps)],
        out_specs=pl.BlockSpec(out_block, out_map),
        out_shape=jax.ShapeDtypeStruct(out_dims, BF16),
        cost_estimate=pl.CostEstimate(flops=flops, bytes_accessed=moved, transcendentals=0),
        compiler_params=pltpu.CompilerParams(vmem_limit_bytes=40 * 1024 * 1024),
    )(*operands)


def lead(i):
    return (i, 0, 0)


def middle_dim(i):
    return (0, i, 0)


def shards(
    held_input,
    fresh_input,
    stashed,
    held_grad,
    fresh_grad,
    first_up,
    second_up,
    first_down,
    second_down,
):
    n = lax.axis_size("blk")
    me = lax.axis_index("blk")
    section_pos = lax.axis_index("section")
    last_section = lax.axis_size("section") - 1
    own_p = FIRST_BLOCKS // n
    own_r = SECOND_BLOCKS // n
    own_groups = own_p // JOIN
    groups = FIRST_BLOCKS // JOIN
    width = JOIN * FIRST_IN
    rows, tokens = held_input.shape[1:]

    def gather(value):
        return lax.all_gather(value, "blk", axis=0, tiled=True)

    up_cut = first_up[0].reshape(2, own_groups, JOIN, FIRST_IN, n, own_r).transpose(4, 1, 0, 5, 2, 3)
    down_cut = second_down[0].reshape(own_groups, JOIN, n, own_r, FIRST_IN).transpose(2, 0, 3, 1, 4)
    cut = jnp.concatenate(
        [
            up_cut.reshape(n, own_groups, 2, own_r, width),
            down_cut.reshape(n, own_groups, 1, own_r, width),
        ],
        axis=2,
    )
    cut = lax.optimization_barrier(cut)
    factors = lax.all_to_all(cut, "blk", split_axis=0, concat_axis=0, tiled=True)
    factors = factors.reshape(groups, 3 * own_r, width)
    up_factor, down_factor = factors[:, : 2 * own_r], factors[:, 2 * own_r :]
    up_second = second_up[0].reshape(2, own_r, FIRST_BLOCKS, -1)
    down_first = first_down[0].reshape(own_r, -1, FIRST_BLOCKS)

    def by_r(factor, values):
        a, t = factor.shape[1], values.shape[1]
        return call(
            by_r_kernel,
            2 * a * FIRST_BLOCKS * width * t,
            (a, FIRST_BLOCKS, t),
            (a, PAIR * JOIN, t),
            middle_dim,
            (factor, values.reshape(groups, width, t)),
            ((PAIR, a, width), (PAIR, width, t)),
            (lead, lead),
        )

    def by_p(factor, values):
        a, _, t = values.shape
        return call(
            by_p_kernel,
            2 * a * FIRST_BLOCKS * width * t,
            (groups, width, t),
            (PAIR, width, t),
            lead,
            (factor, values),
            ((PAIR, a, width), (a, PAIR * JOIN, t)),
            (lead, middle_dim),
        ).reshape(n, rows, t)

    def term_of(values, seen):
        a, _, t = values.shape
        return call(
            functools.partial(term_kernel, factor),
            2 * a * FIRST_BLOCKS * width * t,
            (groups, a, width),
            (PAIR, a, width),
            lead,
            (values, seen.reshape(groups, width, t)),
            ((a, PAIR * JOIN, t), (PAIR, width, t)),
            (middle_dim, lead),
        )

    def middle(values):
        t = values.shape[1]
        spread = by_r(up_factor, values).reshape(2, own_r, FIRST_BLOCKS, t)
        mixed = jnp.einsum("grpo,grpt->grot", up_second, spread, preferred_element_type=F32)
        hidden = (jax.nn.silu(mixed[0]) * mixed[1]).astype(BF16)
        lowered = jnp.einsum("rop,rot->rpt", down_first, hidden, preferred_element_type=F32)
        return spread, mixed, hidden, lowered.astype(BF16)

    def backward(grad_lowered, mixed):
        grad_hidden = jnp.einsum(
            "rop,rpt->rot", down_first, grad_lowered, preferred_element_type=F32
        )
        sg = jax.nn.sigmoid(mixed[0])
        slope = sg * (1.0 + mixed[0] * (1.0 - sg))
        grad_mixed = jnp.stack(
            [grad_hidden * mixed[1] * slope, grad_hidden * mixed[0] * sg]
        ).astype(BF16)
        grad_spread = jnp.einsum(
            "grpo,grot->grpt", up_second, grad_mixed, preferred_element_type=F32
        ).astype(BF16)
        return grad_mixed, grad_spread.reshape(-1, FIRST_BLOCKS, tokens)

    def add(values, added):
        return (values.astype(F32) + added).astype(BF16)

    factor = 1.0 / math.sqrt(TICKS * tokens)
    inputs, grads = held_input[0], held_grad[0]
    inputs_all = gather(inputs)
    grads_all = gather(grads)
    stash_all = gather(jnp.concatenate([stashed[0, k] for k in range(TICKS)], axis=1))
    terms, grads_seen = [], []
    outputs = back = stash = None
    for k in range(TICKS):
        lowered = middle(inputs_all)[3]
        forward_pieces = send(by_p(down_factor, lowered), n, me)
        if stash is None:
            stash_all, _ = lax.optimization_barrier((stash_all, forward_pieces[0]))
            stash = middle(stash_all)
        grad_lowered = by_r(down_factor, grads_all)
        grad_mixed, grad_spread = backward(
            grad_lowered, stash[1][..., k * tokens : (k + 1) * tokens]
        )
        forward_pieces, grad_spread = lax.optimization_barrier((forward_pieces, grad_spread))
        backward_pieces = send(by_p(up_factor, grad_spread), n, me)
        outputs = add(inputs, total_of(forward_pieces))
        terms.append((grad_lowered, grad_mixed, grad_spread))
        grads_seen.append(grads_all)
        if k + 1 < TICKS:
            back = add(grads, total_of(backward_pieces))
            inputs = jnp.where(section_pos == 0, fresh_input, from_behind(outputs, "section", 1))
            grads = jnp.where(
                section_pos == last_section, fresh_grad, from_behind(back, "section", -1)
            )
            inputs_all = gather(inputs)
            grads_all = gather(grads)
    spread, mixed, hidden, lowered = stash
    grad_lowered, grad_mixed, grad_spread = (
        jnp.concatenate([term[i] for term in terms], axis=-1) for i in range(3)
    )
    both = jnp.concatenate(grads_seen, axis=1)

    def finish(total):
        return (total * factor).astype(BF16)

    back_cut = jnp.concatenate([term_of(grad_spread, stash_all), term_of(lowered, both)], axis=1)
    back_cut = back_cut.reshape(n, own_groups, 3, own_r, width)
    small = lax.all_to_all(back_cut, "blk", split_axis=0, concat_axis=0, tiled=True)
    w2 = finish(jnp.einsum("grpt,grot->grpo", spread, grad_mixed, preferred_element_type=F32))
    w3 = finish(jnp.einsum("rot,rpt->rop", hidden, grad_lowered, preferred_element_type=F32))
    back = add(grads, total_of(backward_pieces))
    small = lax.optimization_barrier(small).reshape(n, own_groups, 3, own_r, JOIN, FIRST_IN)
    g1 = small[:, :, :2].transpose(2, 1, 4, 5, 0, 3)
    g4 = small[:, :, 2].transpose(1, 3, 0, 2, 4)
    return (
        outputs.reshape(held_input.shape),
        back.reshape(held_grad.shape),
        g1.reshape(first_up.shape),
        w2.reshape(second_up.shape),
        w3.reshape(first_down.shape),
        g4.reshape(second_down.shape),
    )


def solution(mesh):
    return jax.shard_map(
        shards,
        mesh=mesh,
        in_specs=(
            P("section", "blk", None),
            P("blk", None),
            P("section", None, "blk", None),
            P("section", "blk", None),
            P("blk", None),
            P("section", None, "blk", None),
            P("section", None, "blk", None),
            P("section", "blk", None),
            P("section", "blk", None),
        ),
        out_specs=(
            P("section", "blk", None),
            P("section", "blk", None),
            P("section", None, "blk", None),
            P("section", None, "blk", None),
            P("section", "blk", None),
            P("section", "blk", None),
        ),
        check_vma=False,
    )
```

```python
import math

import jax
import jax.numpy as jnp
from jax import lax
from jax.experimental import pallas as pl
from jax.experimental.pallas import tpu as pltpu
from jax.sharding import PartitionSpec as P

FIRST_BLOCKS = 128
FIRST_IN = 40
SECOND_BLOCKS = 160
PAIR = 2
TICKS = 2
JOIN = 8
F32 = jnp.float32
BF16 = jnp.bfloat16


def partner_of(i, d, n):
    return i ^ d if n & (n - 1) == 0 else (i + d) % n


def source_of(i, d, n):
    return i ^ d if n & (n - 1) == 0 else (i - d) % n


def spread_over(value, n, by):
    sections = lax.axis_size("section")
    arrived = []
    for d in range(n):
        if d == 0 and by == 0:
            arrived.append(value)
            continue
        pairs = [
            (s * n + b, (s + by) % sections * n + partner_of(b, d, n))
            for s in range(sections)
            for b in range(n)
        ]
        arrived.append(lax.ppermute(value, ("section", "blk"), pairs))
    return arrived


def placed(pieces, n, me):
    rows = pieces[0].shape[0]
    whole = jnp.zeros((n * rows,) + pieces[0].shape[1:], pieces[0].dtype)
    for d, piece in enumerate(pieces):
        whole = lax.dynamic_update_slice_in_dim(whole, piece, source_of(me, d, n) * rows, 0)
    return whole


def send(pieces, n, me):
    arrived = [lax.dynamic_index_in_dim(pieces, me, 0, keepdims=False)]
    for d in range(1, n):
        mine = lax.dynamic_index_in_dim(pieces, partner_of(me, d, n), 0, keepdims=False)
        arrived.append(
            lax.ppermute(mine, "blk", [(i, partner_of(i, d, n)) for i in range(n)])
        )
    return arrived


def total_of(pieces):
    return sum(piece.astype(F32) for piece in pieces)


def wide_of(factor):
    a, width = factor.shape
    block = lax.broadcasted_iota(jnp.int32, (JOIN, width), 0) * FIRST_IN
    column = lax.broadcasted_iota(jnp.int32, (JOIN, width), 1)
    keep = (column >= block) & (column < block + FIRST_IN)
    spread = jnp.broadcast_to(factor.astype(F32)[:, None, :], (a, JOIN, width))
    return jnp.where(keep[None], spread, 0.0).reshape(a * JOIN, width)


def by_r_kernel(factor_ref, values_ref, out_ref):
    a = factor_ref.shape[1]
    t = values_ref.shape[2]
    parts = []
    for i in range(PAIR):
        wide = wide_of(factor_ref[i]).astype(BF16)
        out = jnp.dot(wide, values_ref[i], preferred_element_type=F32)
        parts.append(out.reshape(a, JOIN, t))
    out_ref[...] = jnp.concatenate(parts, axis=1).astype(BF16)


def by_p_kernel(factor_ref, rows_ref, out_ref):
    rows = rows_ref[...].astype(F32)
    a, _, t = rows.shape
    for i in range(PAIR):
        wide = wide_of(factor_ref[i]).astype(BF16)
        mine = rows[:, i * JOIN : (i + 1) * JOIN].reshape(a * JOIN, t).astype(BF16)
        out = lax.dot_general(wide, mine, (((0,), (0,)), ((), ())), preferred_element_type=F32)
        out_ref[i] = out.astype(BF16)


def term_kernel(rows_ref, values_ref, out_ref):
    rows = rows_ref[...].astype(F32)
    a, _, t = rows.shape
    width = values_ref.shape[1]
    block = lax.broadcasted_iota(jnp.int32, (JOIN, width), 0) * FIRST_IN
    column = lax.broadcasted_iota(jnp.int32, (JOIN, width), 1)
    keep = (column >= block) & (column < block + FIRST_IN)
    for i in range(PAIR):
        mine = rows[:, i * JOIN : (i + 1) * JOIN].reshape(a * JOIN, t).astype(BF16)
        full = lax.dot_general(
            mine, values_ref[i], (((1,), (1,)), ((), ())), preferred_element_type=F32
        )
        kept = jnp.where(keep[None], full.reshape(a, JOIN, width), 0.0)
        out_ref[i] = jnp.sum(kept, axis=1)


def cut_kernel(up_ref, down_ref, out_ref, low_ref, high_ref):
    owners, count, _, own_r, _ = out_ref.shape
    skip = SECOND_BLOCKS - 128
    for g in range(2):
        x = up_ref[g].astype(F32)
        for i in range(count):
            for q in range(FIRST_IN):
                piece = x[i * JOIN : (i + 1) * JOIN, q * SECOND_BLOCKS : (q + 1) * SECOND_BLOCKS]
                low_ref[pl.ds(q, JOIN, stride=FIRST_IN), :] = piece[:, :128]
                high_ref[pl.ds(q, JOIN, stride=FIRST_IN), :] = piece[:, skip:]
            turned = jnp.concatenate([low_ref[...].T, high_ref[...].T[128 - skip :]], axis=0)
            for o in range(owners):
                out_ref[o, i, g] = turned[o * own_r : (o + 1) * own_r].astype(BF16)
    for i in range(count):
        for o in range(owners):
            out_ref[o, i, 2] = down_ref[o, i, 0]


def join_kernel(cut_ref, out_ref, low_ref, high_ref):
    owners, count, _, own_r, _ = cut_ref.shape
    skip = SECOND_BLOCKS - 128
    for g in range(2):
        parts = []
        for i in range(count):
            x = jnp.concatenate([cut_ref[o, i, g].astype(F32) for o in range(owners)], axis=0)
            low_ref[...] = x[:128].T
            high_ref[...] = x[skip:].T
            pieces = []
            for q in range(FIRST_IN):
                pieces.append(low_ref[pl.ds(q, JOIN, stride=FIRST_IN), :])
                pieces.append(high_ref[pl.ds(q, JOIN, stride=FIRST_IN), :][:, 128 - skip :])
            parts.append(jnp.concatenate(pieces, axis=1))
        out_ref[g] = jnp.concatenate(parts, axis=0).astype(BF16)


def relay_call(kernel, own_p, out_dims, out_block, out_map, operands, blocks, maps):
    return pl.pallas_call(
        kernel,
        grid=(max(own_p // (PAIR * JOIN), 1),),
        in_specs=[pl.BlockSpec(x, m) for x, m in zip(blocks, maps)],
        out_specs=pl.BlockSpec(out_block, out_map),
        out_shape=jax.ShapeDtypeStruct(out_dims, BF16),
        scratch_shapes=[pltpu.VMEM((JOIN * FIRST_IN, 128), F32)] * 2,
        cost_estimate=pl.CostEstimate(
            flops=0, bytes_accessed=math.prod(out_dims) * 4, transcendentals=0
        ),
        compiler_params=pltpu.CompilerParams(vmem_limit_bytes=40 * 1024 * 1024),
    )(*operands)


def call(kernel, flops, out_dims, out_block, out_map, operands, blocks, maps, dtype=BF16):
    moved = sum(x.size for x in operands) * 2 + math.prod(out_dims) * 2
    return pl.pallas_call(
        kernel,
        grid=(FIRST_BLOCKS // (PAIR * JOIN),),
        in_specs=[pl.BlockSpec(x, m) for x, m in zip(blocks, maps)],
        out_specs=pl.BlockSpec(out_block, out_map),
        out_shape=jax.ShapeDtypeStruct(out_dims, dtype),
        cost_estimate=pl.CostEstimate(flops=flops, bytes_accessed=moved, transcendentals=0),
        compiler_params=pltpu.CompilerParams(vmem_limit_bytes=40 * 1024 * 1024),
    )(*operands)


def lead(i):
    return (i, 0, 0)


def middle_dim(i):
    return (0, i, 0)


def shards(
    held_input,
    fresh_input,
    stashed,
    held_grad,
    fresh_grad,
    first_up,
    second_up,
    first_down,
    second_down,
):
    n = lax.axis_size("blk")
    me = lax.axis_index("blk")
    section_pos = lax.axis_index("section")
    last_section = lax.axis_size("section") - 1
    own_p = FIRST_BLOCKS // n
    own_r = SECOND_BLOCKS // n
    own_groups = own_p // JOIN
    groups = FIRST_BLOCKS // JOIN
    width = JOIN * FIRST_IN
    rows, tokens = held_input.shape[1:]

    step = min(PAIR, own_groups)
    five = lambda i: (0, i, 0, 0, 0)
    cut_dims = (n, own_groups, 3, own_r, width)
    cut_block = (n, step, 3, own_r, width)
    down_cut = second_down[0].reshape(own_groups, JOIN, n, own_r, FIRST_IN).transpose(2, 0, 3, 1, 4)
    cut = relay_call(
        cut_kernel,
        own_p,
        cut_dims,
        cut_block,
        five,
        (first_up[0], down_cut.reshape(n, own_groups, 1, own_r, width)),
        ((2, step * JOIN, first_up.shape[3]), (n, step, 1, own_r, width)),
        (middle_dim, five),
    )
    factors = lax.all_to_all(cut, "blk", split_axis=0, concat_axis=0, tiled=True)
    factors = factors.reshape(groups, 3 * own_r, width)
    up_factor, down_factor = factors[:, : 2 * own_r], factors[:, 2 * own_r :]
    up_second = second_up[0].reshape(2, own_r, FIRST_BLOCKS, -1)
    down_first = first_down[0].reshape(own_r, -1, FIRST_BLOCKS)

    def by_r(factor, values):
        a, t = factor.shape[1], values.shape[1]
        return call(
            by_r_kernel,
            2 * a * FIRST_BLOCKS * width * t,
            (a, FIRST_BLOCKS, t),
            (a, PAIR * JOIN, t),
            middle_dim,
            (factor, values.reshape(groups, width, t)),
            ((PAIR, a, width), (PAIR, width, t)),
            (lead, lead),
        )

    def by_p(factor, values):
        a, _, t = values.shape
        return call(
            by_p_kernel,
            2 * a * FIRST_BLOCKS * width * t,
            (groups, width, t),
            (PAIR, width, t),
            lead,
            (factor, values),
            ((PAIR, a, width), (a, PAIR * JOIN, t)),
            (lead, middle_dim),
        ).reshape(n, rows, t)

    def term_of(values, seen):
        a, _, t = values.shape
        return call(
            term_kernel,
            2 * a * FIRST_BLOCKS * width * t,
            (groups, a, width),
            (PAIR, a, width),
            lead,
            (values, seen.reshape(groups, width, t)),
            ((a, PAIR * JOIN, t), (PAIR, width, t)),
            (middle_dim, lead),
            F32,
        )

    def middle(values):
        t = values.shape[1]
        spread = by_r(up_factor, values).reshape(2, own_r, FIRST_BLOCKS, t)
        mixed = jnp.einsum("grpo,grpt->grot", up_second, spread, preferred_element_type=F32)
        hidden = (jax.nn.silu(mixed[0]) * mixed[1]).astype(BF16)
        lowered = jnp.einsum("rop,rot->rpt", down_first, hidden, preferred_element_type=F32)
        return spread, mixed, hidden, lowered.astype(BF16)

    def backward(grad_lowered, mixed):
        grad_hidden = jnp.einsum(
            "rop,rpt->rot", down_first, grad_lowered, preferred_element_type=F32
        )
        sg = jax.nn.sigmoid(mixed[0])
        slope = sg * (1.0 + mixed[0] * (1.0 - sg))
        grad_mixed = jnp.stack(
            [grad_hidden * mixed[1] * slope, grad_hidden * mixed[0] * sg]
        ).astype(BF16)
        grad_spread = jnp.einsum(
            "grpo,grot->grpt", up_second, grad_mixed, preferred_element_type=F32
        ).astype(BF16)
        return grad_mixed, grad_spread.reshape(-1, FIRST_BLOCKS, tokens)

    def add(values, added):
        return (values.astype(F32) + added).astype(BF16)

    factor = 1.0 / math.sqrt(TICKS * tokens)

    def terms_of(stash, stash_all, grads_all, grad_lowered, grad_mixed, grad_spread):
        spread, _, hidden, lowered = stash
        return (
            term_of(grad_spread, stash_all),
            term_of(lowered, grads_all),
            jnp.einsum("grpt,grot->grpo", spread, grad_mixed, preferred_element_type=F32),
            jnp.einsum("rot,rpt->rop", hidden, grad_lowered, preferred_element_type=F32),
        )

    inputs, grads = held_input[0], held_grad[0]
    input_pieces = spread_over(inputs, n, 0)
    grad_pieces = spread_over(grads, n, 0)
    stash_pieces = [
        spread_over(lax.optimization_barrier((stashed[0, k], factors[0]))[0], n, 0)
        for k in range(TICKS)
    ]
    totals = stash = None
    outputs = back = forward_pieces = backward_pieces = None
    for k in range(TICKS):
        lowered = middle(placed(input_pieces, n, me))[3]
        forward_pieces = send(by_p(down_factor, lowered), n, me)
        if k == 0:
            stash_pieces[0], _ = lax.optimization_barrier((stash_pieces[0], forward_pieces[0]))
            stash_all = placed(stash_pieces[0], n, me)
            stash = middle(stash_all)
            forward_pieces, _ = lax.optimization_barrier((forward_pieces, stash[3]))
        outputs = add(inputs, total_of(forward_pieces))
        if k + 1 < TICKS:
            input_pieces = spread_over(
                jnp.where(section_pos == last_section, fresh_input, outputs), n, 1
            )
        grads_all = placed(grad_pieces, n, me)
        grad_lowered = by_r(down_factor, grads_all)
        grad_mixed, grad_spread = backward(grad_lowered, stash[1])
        backward_pieces = send(by_p(up_factor, grad_spread), n, me)
        if k + 1 < TICKS:
            next_pieces, _ = lax.optimization_barrier((stash_pieces[k + 1], backward_pieces[0]))
            next_all = placed(next_pieces, n, me)
            next_stash = middle(next_all)
            input_pieces, backward_pieces, next_stash = lax.optimization_barrier(
                (input_pieces, backward_pieces, next_stash)
            )
            inputs = input_pieces[0]
            back = add(grads, total_of(backward_pieces))
            grad_pieces = spread_over(jnp.where(section_pos == 0, fresh_grad, back), n, -1)
            terms = terms_of(stash, stash_all, grads_all, grad_lowered, grad_mixed, grad_spread)
            totals = terms if totals is None else [x + y for x, y in zip(totals, terms)]
            grad_pieces, totals = lax.optimization_barrier((grad_pieces, totals))
            grads = grad_pieces[0]
            stash, stash_all = next_stash, next_all
    terms = terms_of(stash, stash_all, grads_all, grad_lowered, grad_mixed, grad_spread)
    t1, t4, w2, w3 = (((x + y) * factor).astype(BF16) for x, y in zip(totals, terms))
    back_cut = jnp.concatenate([t1, t4], axis=1).reshape(cut_dims)
    small = lax.all_to_all(back_cut, "blk", split_axis=0, concat_axis=0, tiled=True)
    back = add(grads, total_of(backward_pieces))
    small = lax.optimization_barrier(small)
    g1 = relay_call(
        join_kernel,
        own_p,
        first_up.shape[1:],
        (2, step * JOIN, first_up.shape[3]),
        middle_dim,
        (small,),
        (cut_block,),
        (five,),
    )
    g4 = small[:, :, 2].reshape(n, own_groups, own_r, JOIN, FIRST_IN).transpose(1, 3, 0, 2, 4)
    return (
        outputs.reshape(held_input.shape),
        back.reshape(held_grad.shape),
        g1.reshape(first_up.shape),
        w2.reshape(second_up.shape),
        w3.reshape(first_down.shape),
        g4.reshape(second_down.shape),
    )


def solution(mesh):
    return jax.shard_map(
        shards,
        mesh=mesh,
        in_specs=(
            P("section", "blk", None),
            P("blk", None),
            P("section", None, "blk", None),
            P("section", "blk", None),
            P("blk", None),
            P("section", None, "blk", None),
            P("section", None, "blk", None),
            P("section", "blk", None),
            P("section", "blk", None),
        ),
        out_specs=(
            P("section", "blk", None),
            P("section", "blk", None),
            P("section", None, "blk", None),
            P("section", None, "blk", None),
            P("section", "blk", None),
            P("section", "blk", None),
        ),
        check_vma=False,
    )
```

```python
import functools
import math

import jax
import jax.numpy as jnp
from jax import lax
from jax.experimental import pallas as pl
from jax.experimental.pallas import tpu as pltpu
from jax.sharding import PartitionSpec as P

FIRST_BLOCKS = 128
FIRST_IN = 40
SECOND_BLOCKS = 160
PAIR = 2
TICKS = 2
JOIN = 8
F32 = jnp.float32
BF16 = jnp.bfloat16


def partner_of(i, d, n):
    return i ^ d if n & (n - 1) == 0 else (i + d) % n


def source_of(i, d, n):
    return i ^ d if n & (n - 1) == 0 else (i - d) % n


def spread_over(value, n, by):
    sections = lax.axis_size("section")
    arrived = []
    for d in range(n):
        if d == 0 and by == 0:
            arrived.append(value)
            continue
        pairs = [
            (s * n + b, (s + by) % sections * n + partner_of(b, d, n))
            for s in range(sections)
            for b in range(n)
        ]
        arrived.append(lax.ppermute(value, ("section", "blk"), pairs))
    return arrived


def placed(pieces, n, me):
    rows = pieces[0].shape[0]
    whole = jnp.zeros((n * rows,) + pieces[0].shape[1:], pieces[0].dtype)
    for d, piece in enumerate(pieces):
        whole = lax.dynamic_update_slice_in_dim(whole, piece, source_of(me, d, n) * rows, 0)
    return whole


def send(pieces, n, me):
    arrived = [lax.dynamic_index_in_dim(pieces, me, 0, keepdims=False)]
    for d in range(1, n):
        mine = lax.dynamic_index_in_dim(pieces, partner_of(me, d, n), 0, keepdims=False)
        arrived.append(
            lax.ppermute(mine, "blk", [(i, partner_of(i, d, n)) for i in range(n)])
        )
    return arrived


def total_of(pieces):
    return sum(piece.astype(F32) for piece in pieces)


def wide_of(factor, first, a):
    width = factor.shape[1]
    factor = factor.astype(F32)[first : first + a]
    block = lax.broadcasted_iota(jnp.int32, (JOIN, width), 0) * FIRST_IN
    column = lax.broadcasted_iota(jnp.int32, (JOIN, width), 1)
    keep = (column >= block) & (column < block + FIRST_IN)
    spread = jnp.broadcast_to(factor[:, None, :], (a, JOIN, width))
    return jnp.where(keep[None], spread, 0.0).reshape(a * JOIN, width)


def by_r_kernel(first, factor_ref, values_ref, out_ref):
    a = out_ref.shape[0]
    t = values_ref.shape[2]
    parts = []
    for i in range(PAIR):
        wide = wide_of(factor_ref[i], first, a).astype(BF16)
        out = jnp.dot(wide, values_ref[i], preferred_element_type=F32)
        parts.append(out.reshape(a, JOIN, t))
    out_ref[...] = jnp.concatenate(parts, axis=1).astype(BF16)


def by_p_kernel(first, factor_ref, rows_ref, out_ref):
    rows = rows_ref[...].astype(F32)
    a, _, t = rows.shape
    for i in range(PAIR):
        wide = wide_of(factor_ref[i], first, a).astype(BF16)
        mine = rows[:, i * JOIN : (i + 1) * JOIN].reshape(a * JOIN, t).astype(BF16)
        out = lax.dot_general(wide, mine, (((0,), (0,)), ((), ())), preferred_element_type=F32)
        out_ref[i] = out.astype(BF16)


def term_kernel(rows_ref, values_ref, out_ref):
    rows = rows_ref[...].astype(F32)
    a, _, t = rows.shape
    width = values_ref.shape[1]
    block = lax.broadcasted_iota(jnp.int32, (JOIN, width), 0) * FIRST_IN
    column = lax.broadcasted_iota(jnp.int32, (JOIN, width), 1)
    keep = (column >= block) & (column < block + FIRST_IN)
    for i in range(PAIR):
        mine = rows[:, i * JOIN : (i + 1) * JOIN].reshape(a * JOIN, t).astype(BF16)
        full = lax.dot_general(
            mine, values_ref[i], (((1,), (1,)), ((), ())), preferred_element_type=F32
        )
        kept = jnp.where(keep[None], full.reshape(a, JOIN, width), 0.0)
        out_ref[i] = jnp.sum(kept, axis=1)


def cut_kernel(up_ref, down_ref, out_ref, low_ref, high_ref):
    owners, count, _, own_r, _ = out_ref.shape
    skip = SECOND_BLOCKS - 128
    for g in range(2):
        x = up_ref[g].astype(F32)
        for i in range(count):
            for q in range(FIRST_IN):
                piece = x[i * JOIN : (i + 1) * JOIN, q * SECOND_BLOCKS : (q + 1) * SECOND_BLOCKS]
                low_ref[pl.ds(q, JOIN, stride=FIRST_IN), :] = piece[:, :128]
                high_ref[pl.ds(q, JOIN, stride=FIRST_IN), :] = piece[:, skip:]
            turned = jnp.concatenate([low_ref[...].T, high_ref[...].T[128 - skip :]], axis=0)
            for o in range(owners):
                out_ref[o, i, g] = turned[o * own_r : (o + 1) * own_r].astype(BF16)
    for i in range(count):
        for o in range(owners):
            out_ref[o, i, 2] = down_ref[o, i, 0]


def join_kernel(cut_ref, out_ref, low_ref, high_ref):
    owners, count, _, own_r, _ = cut_ref.shape
    skip = SECOND_BLOCKS - 128
    for g in range(2):
        parts = []
        for i in range(count):
            x = jnp.concatenate([cut_ref[o, i, g].astype(F32) for o in range(owners)], axis=0)
            low_ref[...] = x[:128].T
            high_ref[...] = x[skip:].T
            pieces = []
            for q in range(FIRST_IN):
                pieces.append(low_ref[pl.ds(q, JOIN, stride=FIRST_IN), :])
                pieces.append(high_ref[pl.ds(q, JOIN, stride=FIRST_IN), :][:, 128 - skip :])
            parts.append(jnp.concatenate(pieces, axis=1))
        out_ref[g] = jnp.concatenate(parts, axis=0).astype(BF16)


def relay_call(kernel, own_p, out_dims, out_block, out_map, operands, blocks, maps):
    return pl.pallas_call(
        kernel,
        grid=(max(own_p // (PAIR * JOIN), 1),),
        in_specs=[pl.BlockSpec(x, m) for x, m in zip(blocks, maps)],
        out_specs=pl.BlockSpec(out_block, out_map),
        out_shape=jax.ShapeDtypeStruct(out_dims, BF16),
        scratch_shapes=[pltpu.VMEM((JOIN * FIRST_IN, 128), F32)] * 2,
        cost_estimate=pl.CostEstimate(
            flops=0, bytes_accessed=math.prod(out_dims) * 4, transcendentals=0
        ),
        compiler_params=pltpu.CompilerParams(vmem_limit_bytes=40 * 1024 * 1024),
    )(*operands)


def call(kernel, flops, out_dims, out_block, out_map, operands, blocks, maps, dtype=BF16):
    moved = sum(x.size for x in operands) * 2 + math.prod(out_dims) * 2
    return pl.pallas_call(
        kernel,
        grid=(FIRST_BLOCKS // (PAIR * JOIN),),
        in_specs=[pl.BlockSpec(x, m) for x, m in zip(blocks, maps)],
        out_specs=pl.BlockSpec(out_block, out_map),
        out_shape=jax.ShapeDtypeStruct(out_dims, dtype),
        cost_estimate=pl.CostEstimate(flops=flops, bytes_accessed=moved, transcendentals=0),
        compiler_params=pltpu.CompilerParams(vmem_limit_bytes=40 * 1024 * 1024),
    )(*operands)


def backward_kernel(mixed_ref, grad_ref, up_ref, down_ref, out_mixed_ref, out_ref):
    for r in range(grad_ref.shape[0]):
        gate, up = mixed_ref[0, r], mixed_ref[1, r]
        grad_hidden = jnp.dot(down_ref[r], grad_ref[r], preferred_element_type=F32)
        sg = 1.0 / (1.0 + jnp.exp(-gate))
        pair = (grad_hidden * up * (sg * (1.0 + gate * (1.0 - sg))), grad_hidden * gate * sg)
        for g in range(2):
            turned = pair[g].astype(BF16)
            out_mixed_ref[g, r] = turned
            out = jnp.dot(up_ref[g, r], turned, preferred_element_type=F32)
            out_ref[g, r] = out.astype(BF16)


def weight_kernel(factor, *refs):
    half = (len(refs) - 2) // 2
    out_ref, held_ref = refs[-2:]
    count, high, _ = refs[0].shape
    for a in range(count):
        left = jnp.concatenate([ref[a] for ref in refs[:half]], axis=1)
        right = jnp.concatenate([ref[a] for ref in refs[half : 2 * half]], axis=1)
        held_ref[a * high : (a + 1) * high] = factor * lax.dot_general(
            left, right, (((1,), (1,)), ((), ())), preferred_element_type=F32
        )
    wide = held_ref.shape[1]
    for m in range(high):
        row = held_ref[pl.ds(m, count, stride=high), :]
        out_ref[:, m * wide : (m + 1) * wide] = row.astype(BF16)


def weight_call(lefts, rights, factor):
    total, high, t = lefts[0].shape
    wide = rights[0].shape[1]
    count = 16 if total % 16 == 0 else total
    return pl.pallas_call(
        functools.partial(weight_kernel, factor),
        grid=(total // count,),
        in_specs=[pl.BlockSpec((count,) + x.shape[1:], lead) for x in (*lefts, *rights)],
        out_specs=pl.BlockSpec((count, high * wide), lambda i: (i, 0)),
        out_shape=jax.ShapeDtypeStruct((total, high * wide), BF16),
        scratch_shapes=[pltpu.VMEM((count * high, wide), F32)],
        cost_estimate=pl.CostEstimate(
            flops=2 * len(lefts) * total * high * wide * t,
            bytes_accessed=2 * total * (high * wide + 2 * len(lefts) * high * t),
            transcendentals=0,
        ),
        compiler_params=pltpu.CompilerParams(vmem_limit_bytes=48 * 1024 * 1024),
    )(*lefts, *rights)


def lead(i):
    return (i, 0, 0)


def middle_dim(i):
    return (0, i, 0)


def shards(
    held_input,
    fresh_input,
    stashed,
    held_grad,
    fresh_grad,
    first_up,
    second_up,
    first_down,
    second_down,
):
    n = lax.axis_size("blk")
    me = lax.axis_index("blk")
    section_pos = lax.axis_index("section")
    last_section = lax.axis_size("section") - 1
    own_p = FIRST_BLOCKS // n
    own_r = SECOND_BLOCKS // n
    own_groups = own_p // JOIN
    groups = FIRST_BLOCKS // JOIN
    width = JOIN * FIRST_IN
    rows, tokens = held_input.shape[1:]

    step = min(PAIR, own_groups)
    five = lambda i: (0, i, 0, 0, 0)
    cut_dims = (n, own_groups, 3, own_r, width)
    cut_block = (n, step, 3, own_r, width)
    down_cut = second_down[0].reshape(own_groups, JOIN, n, own_r, FIRST_IN).transpose(2, 0, 3, 1, 4)
    cut = relay_call(
        cut_kernel,
        own_p,
        cut_dims,
        cut_block,
        five,
        (first_up[0], down_cut.reshape(n, own_groups, 1, own_r, width)),
        ((2, step * JOIN, first_up.shape[3]), (n, step, 1, own_r, width)),
        (middle_dim, five),
    )
    factors = lax.all_to_all(cut, "blk", split_axis=0, concat_axis=0, tiled=True)
    factors = factors.reshape(groups, 3 * own_r, width)
    up_factor, down_factor = (0, 2 * own_r), (2 * own_r, own_r)
    up_second = second_up[0].reshape(2, own_r, FIRST_BLOCKS, -1)
    down_first = first_down[0].reshape(own_r, -1, FIRST_BLOCKS)

    def by_r(factor, values):
        (first, a), t = factor, values.shape[1]
        return call(
            functools.partial(by_r_kernel, first),
            2 * a * FIRST_BLOCKS * width * t,
            (a, FIRST_BLOCKS, t),
            (a, PAIR * JOIN, t),
            middle_dim,
            (factors, values.reshape(groups, width, t)),
            ((PAIR, 3 * own_r, width), (PAIR, width, t)),
            (lead, lead),
        )

    def by_p(factor, values):
        a, _, t = values.shape
        return call(
            functools.partial(by_p_kernel, factor[0]),
            2 * a * FIRST_BLOCKS * width * t,
            (groups, width, t),
            (PAIR, width, t),
            lead,
            (factors, values),
            ((PAIR, 3 * own_r, width), (a, PAIR * JOIN, t)),
            (lead, middle_dim),
        ).reshape(n, rows, t)

    def term_of(values, seen):
        a, _, t = values.shape
        return call(
            term_kernel,
            2 * a * FIRST_BLOCKS * width * t,
            (groups, a, width),
            (PAIR, a, width),
            lead,
            (values, seen.reshape(groups, width, t)),
            ((a, PAIR * JOIN, t), (PAIR, width, t)),
            (middle_dim, lead),
            F32,
        )

    def middle(values):
        t = values.shape[1]
        spread = by_r(up_factor, values).reshape(2, own_r, FIRST_BLOCKS, t)
        mixed = jnp.einsum("grpo,grpt->grot", up_second, spread, preferred_element_type=F32)
        hidden = (jax.nn.silu(mixed[0]) * mixed[1]).astype(BF16)
        lowered = jnp.einsum("rop,rot->rpt", down_first, hidden, preferred_element_type=F32)
        return spread, mixed, hidden, lowered.astype(BF16)

    def backward(grad_lowered, mixed):
        count = 8 if own_r % 8 == 0 else own_r
        four = lambda i: (0, i, 0, 0)
        wide = mixed.shape[2]
        shapes = ((2, own_r, wide, tokens), (2, own_r, FIRST_BLOCKS, tokens))
        grad_mixed, grad_spread = pl.pallas_call(
            backward_kernel,
            grid=(own_r // count,),
            in_specs=[
                pl.BlockSpec((2, count, wide, tokens), four),
                pl.BlockSpec((count, FIRST_BLOCKS, tokens), lead),
                pl.BlockSpec((2, count, FIRST_BLOCKS, wide), four),
                pl.BlockSpec((count, wide, FIRST_BLOCKS), lead),
            ],
            out_specs=[pl.BlockSpec((2, count) + x[2:], four) for x in shapes],
            out_shape=[jax.ShapeDtypeStruct(x, BF16) for x in shapes],
            cost_estimate=pl.CostEstimate(
                flops=6 * own_r * FIRST_BLOCKS * wide * tokens,
                bytes_accessed=20 * own_r * wide * tokens,
                transcendentals=own_r * wide * tokens,
            ),
            compiler_params=pltpu.CompilerParams(vmem_limit_bytes=40 * 1024 * 1024),
        )(mixed, grad_lowered, up_second, down_first)
        return grad_mixed, grad_spread.reshape(-1, FIRST_BLOCKS, tokens)

    def add(values, added):
        return (values.astype(F32) + added).astype(BF16)

    factor = 1.0 / math.sqrt(TICKS * tokens)

    def terms_of(stash, stash_all, grads_all, grad_spread):
        return term_of(grad_spread, stash_all), term_of(stash[3], grads_all)

    inputs, grads = held_input[0], held_grad[0]
    input_pieces = spread_over(inputs, n, 0)
    grad_pieces = spread_over(lax.optimization_barrier((grads, factors[0]))[0], n, 0)
    stash_pieces = [
        spread_over(lax.optimization_barrier((stashed[0, k], factors[0]))[0], n, 0)
        for k in range(TICKS)
    ]
    totals = stash = None
    seen = []
    outputs = back = forward_pieces = backward_pieces = None
    for k in range(TICKS):
        lowered = middle(placed(input_pieces, n, me))[3]
        forward_pieces = send(by_p(down_factor, lowered), n, me)
        if k == 0:
            stash_pieces[0], _ = lax.optimization_barrier((stash_pieces[0], forward_pieces[0]))
            stash_all = placed(stash_pieces[0], n, me)
            stash = middle(stash_all)
            forward_pieces, _ = lax.optimization_barrier((forward_pieces, stash[3]))
        outputs = add(inputs, total_of(forward_pieces))
        if k + 1 < TICKS:
            input_pieces = spread_over(
                jnp.where(section_pos == last_section, fresh_input, outputs), n, 1
            )
        grads_all = placed(grad_pieces, n, me)
        grad_lowered = by_r(down_factor, grads_all)
        grad_mixed, grad_spread = backward(grad_lowered, stash[1])
        pieces = by_p(up_factor, grad_spread)
        backward_pieces = send(pieces, n, me)
        seen.append((stash[0].reshape(-1, FIRST_BLOCKS, tokens), stash[2], grad_lowered, grad_mixed))
        if k + 1 < TICKS:
            next_pieces, _ = lax.optimization_barrier((stash_pieces[k + 1], backward_pieces[0]))
            next_all = placed(next_pieces, n, me)
            next_stash = middle(next_all)
            input_pieces, backward_pieces, next_stash = lax.optimization_barrier(
                (input_pieces, backward_pieces, next_stash)
            )
            inputs = input_pieces[0]
            back = add(grads, total_of(backward_pieces))
            grad_pieces = spread_over(jnp.where(section_pos == 0, fresh_grad, back), n, -1)
            terms = terms_of(stash, stash_all, grads_all, grad_spread)
            totals = terms if totals is None else [x + y for x, y in zip(totals, terms)]
            grad_pieces, totals = lax.optimization_barrier((grad_pieces, totals))
            grads = grad_pieces[0]
            stash, stash_all = next_stash, next_all
    grad_spread, _ = lax.optimization_barrier((grad_spread, pieces))
    terms = terms_of(stash, stash_all, grads_all, grad_spread)
    t1, t4 = (((x + y) * factor).astype(BF16) for x, y in zip(totals, terms))
    back_cut = jnp.concatenate([t1, t4], axis=1).reshape(cut_dims)
    seen, back_cut = lax.optimization_barrier((seen, back_cut))
    spreads, hiddens, grads_lowered, grads_mixed = zip(*seen)
    grads_mixed = [x.reshape(2 * own_r, -1, tokens) for x in grads_mixed]
    small = lax.all_to_all(back_cut, "blk", split_axis=0, concat_axis=0, tiled=True)
    w2 = weight_call(spreads, grads_mixed, factor)
    w3 = weight_call(hiddens, grads_lowered, factor)
    small, backward_pieces, w2, w3 = lax.optimization_barrier((small, backward_pieces, w2, w3))
    back = add(grads, total_of(backward_pieces))
    small = lax.optimization_barrier(small)
    g1 = relay_call(
        join_kernel,
        own_p,
        first_up.shape[1:],
        (2, step * JOIN, first_up.shape[3]),
        middle_dim,
        (small,),
        (cut_block,),
        (five,),
    )
    g4 = small[:, :, 2].reshape(n, own_groups, own_r, JOIN, FIRST_IN).transpose(1, 3, 0, 2, 4)
    return (
        outputs.reshape(held_input.shape),
        back.reshape(held_grad.shape),
        g1.reshape(first_up.shape),
        w2.reshape(second_up.shape),
        w3.reshape(first_down.shape),
        g4.reshape(second_down.shape),
    )


def solution(mesh):
    return jax.shard_map(
        shards,
        mesh=mesh,
        in_specs=(
            P("section", "blk", None),
            P("blk", None),
            P("section", None, "blk", None),
            P("section", "blk", None),
            P("blk", None),
            P("section", None, "blk", None),
            P("section", None, "blk", None),
            P("section", "blk", None),
            P("section", "blk", None),
        ),
        out_specs=(
            P("section", "blk", None),
            P("section", "blk", None),
            P("section", None, "blk", None),
            P("section", None, "blk", None),
            P("section", "blk", None),
            P("section", "blk", None),
        ),
        check_vma=False,
    )
```
